512 devices in a mesh: gx: 32 (over z, y_hi), gy: 4 (over y_lo, core), gz: 4 (over x).
Axes of the slice: x: 4, y: 8 (y_hi: 4, y_lo: 2; y = y_hi * 2 + y_lo), z: 8, core: 2. Of those that a mesh axis runs over, the one named last changes fastest.
Arguments:
- activations: bfloat16 [128, 8192], P(None, ('gx', 'gy', 'gz')), may hold values from -24 to 24
- w_qkv: bfloat16 [8192, 10240], P('gx', ('gy', 'gz')), may hold values from -0.0625 to 0.0625
- k_cache: bfloat16 [128, 4096, 8, 128], P(('gx', 'gz'), None, 'gy'), may hold values from -1000 to 1000
- v_cache: bfloat16 [128, 4096, 8, 128], P(('gx', 'gz'), None, 'gy'), may hold values from -6 to 6
- lengths: int32 [128], P(('gx', 'gz')), may hold values from 256 to 4096, as said below
- w_out: bfloat16 [8192, 8192], P(('gy', 'gz'), 'gx'), may hold values from -0.125 to 0.125
Outputs:
- update: bfloat16 [128, 8192], P(None, ('gx', 'gy', 'gz'))
The draws below stay inside these ranges and needn't reach their ends.
Inputs may be any that keep to these rules, and one draw needn't show every extreme that they name: `lengths`: some sequence has exactly 4096 cached tokens.
All inputs are finite; a program needn't handle non-finite values.
Results may differ from the reference program's by a relative error of at most 0.0085.
The reference program's roundings to bfloat16 on the way (of `mixed`, `queries`, `weights` and `attended`) count: a program that leaves them out, or rounds other values in their place, can miss the bound.
Values may be sent and summed in bfloat16 or wider, within the bound.
No kernel may reach another device: no remote copies, remote signals or barrier semaphores. Data moves between devices by JAX's collectives and lax.ppermute only.
A program may use at most 64 MiB of HBM per device.

```python
import math
import jax
import jax.numpy as jnp
from jax import lax

D = 8192
QH = 64
KVH = 8
HD = 128
S = 4096
SEQS = 128
QKV = 10240


def draw_k_cache(key, part):
    key = jax.random.fold_in(key, 11)
    shape = (SEQS, S, KVH, HD)
    return jnp.clip(jax.random.normal(key, shape, jnp.float32), -6.0, 6.0).astype(jnp.bfloat16)


def draw_lengths(key, part):
    key = jax.random.fold_in(key, 23)
    lowest = max(2, S // 16)
    drawn = jax.random.randint(key, (SEQS,), lowest, S + 1, dtype=jnp.int32)
    longest = jax.random.randint(jax.random.fold_in(key, 1), (), 0, SEQS, dtype=jnp.int32)
    return drawn.at[longest].set(S)


def raised(values, rng, source, target, shards_of, factor):
    def block_of(axis_at):
        return (jnp.arange(values.shape[axis_at]) // (values.shape[axis_at] // shards_of)).reshape((-1,) + (1,) * (values.ndim - 1 - axis_at))

    near = jax.random.permutation(rng, shards_of)[block_of(target)]
    far = (block_of(target) + shards_of // 2) % shards_of
    return jnp.where((block_of(source) == near) | (block_of(source) == far), factor * values, values)


def block_scale(rng, dims, pieces, low, top_value):
    factor_of, own = 1.0, jax.random.fold_in(rng, 6)
    for dim, parts in pieces:
        draws = jnp.exp(jax.random.uniform(jax.random.fold_in(own, dim), (parts,), jnp.float32, low / len(pieces), top_value / len(pieces)))
        factor_of = factor_of * jnp.repeat(draws, dims[dim] // parts).reshape([-1 if axis == dim else 1 for axis in range(len(dims))])
    return factor_of


def noise(key, dims, width, bound, split=(), kind=jnp.bfloat16):
    values = width * jax.random.normal(key, dims, jnp.float32)
    if split:
        values = values * block_scale(key, dims, split, -0.22, 0.18)
    return jnp.clip(values, -bound, bound).astype(kind)


def gaussian_with(key, dims, scale, most, pieces, heavy, kind=jnp.bfloat16):
    result = scale * jax.random.normal(key, dims, jnp.float32)
    if pieces:
        result = result * block_scale(key, dims, pieces, -0.22, 0.18)
    return jnp.clip(raised(result, jax.random.fold_in(key, 3), *heavy), -most, most).astype(kind)


def setup_inputs(seed: int = 0) -> dict:
    seeds = jax.random.split(jax.random.key(seed), 7)
    return {
        "activations": gaussian_with(seeds[0], (SEQS, D), 1.0, 24.0, ((1, 512),), (1, 0, 128, 5.5)),
        "w_qkv": noise(seeds[1], (D, QKV), D ** -0.5, 0.0625, ((0, 32), (1, 16))),
        "k_cache": draw_k_cache(jax.random.fold_in(seeds[6], 71), 0),
        "v_cache": noise(seeds[3], (SEQS, S, KVH, HD), 1.0, 6.0, ((0, 128), (2, 4))),
        "lengths": draw_lengths(jax.random.fold_in(seeds[6], 71), 0),
        "w_out": gaussian_with(seeds[5], (QH * HD, D), (QH * HD) ** -0.5, 0.125, ((0, 16), (1, 32)), (0, 1, 32, 2.75)),
    }


ROPE_BASE = 500000.0

def rotate(values, position):
    half_dim = values.shape[-1] // 2
    freqs = jnp.exp(jnp.arange(half_dim, dtype=jnp.float32) * (-2.0 * math.log(ROPE_BASE) / values.shape[-1]))
    angles = position * freqs
    cosine = jnp.cos(angles)
    sine = jnp.sin(angles)
    first_half = values[..., :half_dim]
    second_half = values[..., half_dim:]
    return jnp.concatenate([first_half * cosine - second_half * sine, second_half * cosine + first_half * sine], axis=-1)

def reference(activations, w_qkv, k_cache, v_cache, lengths, w_out):
    mixed = jnp.dot(activations, w_qkv, preferred_element_type=jnp.float32).astype(jnp.bfloat16)
    per_half = QH // (2 * KVH)
    blocks = mixed.reshape(SEQS, KVH, 2, per_half + 1, HD)
    queries_all = blocks[:, :, :, :per_half].reshape(SEQS, KVH, 2 * per_half, HD)
    keys_new = blocks[:, :, 0, per_half]
    values_new = blocks[:, :, 1, per_half]
    score_scale = 1.0 / math.sqrt(HD)

    def one_sequence(operands):
        queries, key_new, value_new, keys_old, values_old, length = operands
        place = length.astype(jnp.float32)
        queries = rotate(queries.astype(jnp.float32), place).astype(jnp.bfloat16)
        key_new = rotate(key_new.astype(jnp.float32), place).astype(jnp.bfloat16)
        scores = jnp.einsum('ghd,sgd->ghs', queries.astype(jnp.float32), keys_old.astype(jnp.float32)) * score_scale
        live = jnp.arange(S, dtype=jnp.int32) < length
        scores = jnp.where(live[None, None, :], scores, -jnp.inf)
        own_score = jnp.einsum('ghd,gd->gh', queries.astype(jnp.float32), key_new.astype(jnp.float32)) * score_scale
        highest = jnp.maximum(lax.optimization_barrier(jnp.max(scores, axis=-1)), own_score)
        exponent = jnp.exp(scores - highest[..., None])
        own_exponent = jnp.exp(own_score - highest)
        denominator = lax.optimization_barrier(jnp.sum(exponent, axis=-1)) + own_exponent
        weights = (exponent / denominator[..., None]).astype(jnp.bfloat16)
        own_weight = (own_exponent / denominator).astype(jnp.bfloat16)
        attended = jnp.einsum('ghs,sgd->ghd', weights.astype(jnp.float32), values_old.astype(jnp.float32))
        attended = attended + own_weight.astype(jnp.float32)[..., None] * value_new.astype(jnp.float32)[:, None, :]
        return attended.astype(jnp.bfloat16).reshape(-1)
    attended_all = lax.map(one_sequence, (queries_all, keys_new, values_new, k_cache, v_cache, lengths))
    return jnp.dot(attended_all, w_out, preferred_element_type=jnp.float32).astype(jnp.bfloat16)
```

```python
import math

import jax
import jax.numpy as jnp
from jax import lax
from jax.sharding import PartitionSpec as P

ROPE_BASE = 500000.0


def rotate(values, position):
    half_dim = values.shape[-1] // 2
    freqs = jnp.exp(
        jnp.arange(half_dim, dtype=jnp.float32) * (-2.0 * math.log(ROPE_BASE) / values.shape[-1])
    )
    angles = position * freqs
    cosine = jnp.cos(angles)
    sine = jnp.sin(angles)
    first_half = values[..., :half_dim]
    second_half = values[..., half_dim:]
    return jnp.concatenate(
        [first_half * cosine - second_half * sine, second_half * cosine + first_half * sine],
        axis=-1,
    )


def exchange(values, axes):
    return lax.all_to_all(values, axes, split_axis=0, concat_axis=0, tiled=True)


def shards(activations, w_qkv, k_cache, v_cache, lengths, w_out):
    out_cols = w_qkv.shape[1]
    groups = k_cache.shape[2]
    head_dim = k_cache.shape[3]
    span = k_cache.shape[1]
    per_half = out_cols // head_dim - 1
    heads_here = 2 * per_half
    mine_t = exchange(jnp.broadcast_to(activations.T, (16,) + activations.T.shape), ("gy", "gz"))
    partial_terms = jnp.einsum(
        "ks,kn->sn",
        mine_t.reshape(-1, mine_t.shape[-1]),
        w_qkv,
        preferred_element_type=jnp.float32,
    )
    rows = partial_terms.shape[0]
    sent = partial_terms.reshape(rows, out_cols // head_dim, 1, head_dim)
    received = exchange(sent, ("gx", "gz"))
    local_row = jnp.sum(
        received.reshape(32, 4, out_cols // head_dim, head_dim), axis=0
    ).astype(jnp.bfloat16)
    blocks = local_row.reshape(groups, 2, per_half + 1, head_dim)
    position = lengths[0]
    place = position.astype(jnp.float32)
    queries = rotate(
        blocks[:, :, :per_half].reshape(groups, heads_here, head_dim).astype(jnp.float32), place
    ).astype(jnp.bfloat16)
    key_new = rotate(blocks[:, 0, per_half].astype(jnp.float32), place).astype(jnp.bfloat16)
    value_new = blocks[:, 1, per_half]
    score_scale = 1.0 / math.sqrt(head_dim)
    keys_old = k_cache[0]
    values_old = v_cache[0]
    own_score = (
        jnp.einsum("ghd,gd->gh", queries, key_new, preferred_element_type=jnp.float32) * score_scale
    )
    scores = (
        jnp.einsum("ghd,sgd->ghs", queries, keys_old, preferred_element_type=jnp.float32)
        * score_scale
    )
    spots = lax.broadcasted_iota(jnp.int32, (1, 1, span), 2)
    scores = jnp.where(spots < position, scores, -jnp.inf)
    highest = jnp.maximum(jnp.max(scores, axis=-1), own_score)
    exponent = jnp.exp(scores - highest[..., None])
    own_exponent = jnp.exp(own_score - highest)
    denominator = jnp.sum(exponent, axis=-1) + own_exponent
    weights = (exponent / denominator[..., None]).astype(jnp.bfloat16)
    own_weight = (own_exponent / denominator).astype(jnp.bfloat16)
    new_term = own_weight.astype(jnp.float32)[..., None] * value_new.astype(jnp.float32)[:, None, :]
    attended = new_term + jnp.einsum(
        "ghs,sgd->ghd", weights, values_old, preferred_element_type=jnp.float32
    )
    w_rows = lax.all_gather(w_out, "gz", axis=0, tiled=True)
    heads = groups * heads_here
    pieces = attended.astype(jnp.bfloat16).reshape(heads, head_dim)
    mine = exchange(jnp.broadcast_to(pieces, (32, heads, head_dim)), "gx")
    ours = lax.broadcasted_iota(jnp.int32, (1, 4, 1, 1), 1) == lax.axis_index("gz")
    spread = jnp.where(ours, mine[:, None], 0).astype(jnp.bfloat16)
    out_terms = jnp.einsum(
        "sk,kn->ns",
        spread.reshape(rows, heads * head_dim),
        w_rows,
        preferred_element_type=jnp.float32,
    )
    out_parts = exchange(out_terms.reshape(16, -1, rows), ("gy", "gz"))
    return jnp.sum(out_parts, axis=0).astype(jnp.bfloat16).T


def solution(mesh):
    placed = (
        P(None, ("gx", "gy", "gz")),
        P("gx", ("gy", "gz")),
        P(("gx", "gz"), None, "gy", None),
        P(("gx", "gz"), None, "gy", None),
        P(("gx", "gz")),
        P(("gy", "gz"), "gx"),
    )
    return jax.shard_map(
        shards, mesh=mesh, in_specs=placed, out_specs=P(None, ("gx", "gy", "gz")), check_vma=False
    )
```

```python
import math

import jax
import jax.numpy as jnp
from jax import lax
from jax.experimental import pallas as pl
from jax.experimental.pallas import tpu as pltpu
from jax.sharding import Mesh
from jax.sharding import PartitionSpec as P

ROPE_BASE = 500000.0
LANES = 128
KEYS_STEP = 2048
EARLY = 3072
WIDTH = ("z", "yh")
GROUPS = ("yl", "core")
HEADS = GROUPS + ("x",)
SEQUENCES = WIDTH + ("x",)


def exchange(values, axes):
    return lax.all_to_all(values, axes, split_axis=0, concat_axis=0, tiled=True)


def load(values_ref, weights_ref, copies_ref, held_ref, first_ref, sems):
    weights = pltpu.make_async_copy(weights_ref, held_ref, sems.at[0])
    values = pltpu.make_async_copy(values_ref, first_ref, sems.at[1])
    values.start()
    weights.start()
    values.wait()
    copies_ref[...] = jnp.broadcast_to(first_ref[...][None], copies_ref.shape)
    weights.wait()


def in_hbm(values):
    return pltpu.with_memory_space_constraint(values, pltpu.HBM)


def fetch(
    length_ref,
    after_ref,
    keys_ref,
    values_ref,
    held_keys_ref,
    held_values_ref,
    turns_ref,
    sems,
):
    size = held_values_ref.shape[0]
    copies = [
        pltpu.make_async_copy(keys_ref, held_keys_ref, sems.at[0]),
        pltpu.make_async_copy(values_ref.at[pl.ds(0, size), :], held_values_ref, sems.at[1]),
    ]
    for copy in copies:
        copy.start()
    lane = lax.broadcasted_iota(jnp.int32, (8, LANES), 1)
    half = LANES // 2
    first = lane < half
    spot = jnp.where(first, lane, lane - half).astype(jnp.float32)
    freqs = jnp.exp(spot * (-2.0 * math.log(ROPE_BASE) / LANES))
    angles = length_ref[0].astype(jnp.float32) * freqs
    sine = jnp.sin(angles)
    turns_ref[0] = jnp.cos(angles)
    turns_ref[1] = jnp.where(first, -sine, sine)
    for copy in copies:
        copy.wait()


def project(mine_ref, weights_ref, out_ref, terms_ref):
    rows = mine_ref.shape[1]
    terms = lax.dot_general(
        mine_ref[...],
        weights_ref[...],
        (((0,), (0,)), ((), ())),
        preferred_element_type=jnp.float32,
    )
    pieces = terms.shape[1] // LANES
    for piece in range(pieces):
        terms_ref[pl.ds(piece * rows, rows), :] = terms[:, piece * LANES : (piece + 1) * LANES]
    deep, near = 8, 4
    wide = rows // deep
    for place in range(wide):
        first = (place // near) * deep * near + place % near
        for piece in range(pieces):
            out_ref[pl.ds(first * pieces + piece, deep, stride=near * pieces), :] = terms_ref[
                pl.ds(piece * rows + place, deep, stride=wide), :
            ]


def attend(
    length_ref,
    turns_ref,
    received_ref,
    keys_ref,
    early_ref,
    values_ref,
    out_ref,
    queries_ref,
    scores_ref,
    held_ref,
    sems,
):
    early = early_ref.shape[0]
    late = values_ref.shape[0] - early
    copies = [
        pltpu.make_async_copy(
            values_ref.at[pl.ds(early, late), :], held_ref.at[pl.ds(early, late), :], sems.at[0]
        ),
        pltpu.make_async_copy(early_ref, held_ref.at[pl.ds(0, early), :], sems.at[1]),
    ]
    for copy in copies:
        copy.start()
    groups = 2
    length = length_ref[0]
    blocks = 4
    rows = received_ref.shape[0] // 32
    pieces = rows // blocks
    heads = pieces - 1
    sums = jnp.sum(received_ref[...].reshape(16, 2 * rows, LANES), axis=0)
    mixed = sums[:rows] + sums[rows:]
    mixed = mixed.astype(jnp.bfloat16).astype(jnp.float32)
    turned = mixed * turns_ref[0, :1] + pltpu.roll(mixed, LANES // 2, 1) * turns_ref[1, :1]
    turned = turned.astype(jnp.bfloat16).astype(jnp.float32)
    for block in range(blocks):
        queries_ref[pl.ds(block * heads, heads), :] = turned[
            block * pieces : block * pieces + heads
        ]
    queries = queries_ref[...]

    def new(values, block):
        return values[block * pieces + heads : (block + 1) * pieces]

    scale = 1.0 / math.sqrt(LANES)
    row_group = lax.broadcasted_iota(jnp.int32, (4 * heads, 1), 0) // (2 * heads)
    key_new = jnp.where(row_group == 0, new(turned, 0), new(turned, 2))
    value_new = jnp.where(row_group == 0, new(mixed, 1), new(mixed, 3))
    own = jnp.sum(queries * key_new, axis=1, keepdims=True) * scale
    queries = queries.astype(jnp.bfloat16)
    span = keys_ref.shape[0]
    steps = span // KEYS_STEP
    column = lax.broadcasted_iota(jnp.int32, (4 * heads, KEYS_STEP), 1)
    same = (column % groups) == row_group
    place = jnp.where(same, column, groups * span)
    top = own
    for step in range(steps):
        block = pl.ds(step * KEYS_STEP, KEYS_STEP)
        scores = lax.dot_general(
            queries,
            keys_ref[block, :],
            (((1,), (1,)), ((), ())),
            preferred_element_type=jnp.float32,
        ) * scale
        scores = jnp.where(place < groups * length - step * KEYS_STEP, scores, -jnp.inf)
        scores_ref[:, block] = scores
        top = jnp.maximum(top, jnp.max(scores, axis=1, keepdims=True))
    own = jnp.exp(own - top)
    total = own
    for step in range(steps):
        block = pl.ds(step * KEYS_STEP, KEYS_STEP)
        exponent = jnp.exp(scores_ref[:, block] - top)
        scores_ref[:, block] = exponent
        total = total + jnp.sum(exponent, axis=1, keepdims=True)
    inverse = 1.0 / total
    own = (own * inverse).astype(jnp.bfloat16).astype(jnp.float32)
    attended = own * value_new
    for copy in copies:
        copy.wait()
    for step in range(steps):
        block = pl.ds(step * KEYS_STEP, KEYS_STEP)
        weights = (scores_ref[:, block] * inverse).astype(jnp.bfloat16)
        attended = attended + jnp.dot(
            weights, held_ref[block, :], preferred_element_type=jnp.float32
        )
    out_ref[...] = jnp.broadcast_to(attended.astype(jnp.bfloat16)[None], out_ref.shape)


def shards(activations, w_qkv, k_cache, v_cache, lengths, w_out):
    out_cols = w_qkv.shape[1]
    head_dim = k_cache.shape[3]
    rows = activations.shape[0]
    vmem = pl.BlockSpec(memory_space=pltpu.VMEM)
    hbm = pl.BlockSpec(memory_space=pltpu.HBM)
    anywhere = pl.BlockSpec(memory_space=pl.ANY)
    pieces = out_cols // head_dim
    copies, weights = pl.pallas_call(
        load,
        out_shape=(
            jax.ShapeDtypeStruct((16,) + activations.T.shape, activations.dtype),
            jax.ShapeDtypeStruct(w_qkv.shape, w_qkv.dtype),
        ),
        in_specs=[hbm, hbm],
        out_specs=(vmem, vmem),
        scratch_shapes=[
            pltpu.VMEM(activations.T.shape, activations.dtype),
            pltpu.SemaphoreType.DMA((2,)),
        ],
        compiler_params=pltpu.CompilerParams(vmem_limit_bytes=4 * 2**20),
    )(in_hbm(activations.T), in_hbm(w_qkv))
    mine_t = exchange(copies, HEADS)
    sent = pl.pallas_call(
        project,
        out_shape=jax.ShapeDtypeStruct((rows * pieces, head_dim), jnp.float32),
        in_specs=[vmem, vmem],
        out_specs=vmem,
        scratch_shapes=[pltpu.VMEM((rows * pieces, head_dim), jnp.float32)],
        compiler_params=pltpu.CompilerParams(vmem_limit_bytes=4 * 2**20),
    )(mine_t.reshape(-1, rows), weights)
    span = k_cache.shape[1] * k_cache.shape[2]
    cache = jax.ShapeDtypeStruct((span, head_dim), k_cache.dtype)
    early_cache = jax.ShapeDtypeStruct((EARLY, head_dim), v_cache.dtype)
    old_values = in_hbm(v_cache.reshape(span, head_dim))
    smem = pl.BlockSpec(memory_space=pltpu.SMEM)
    keys, early, turns = pl.pallas_call(
        fetch,
        out_shape=(cache, early_cache, jax.ShapeDtypeStruct((2, 8, LANES), jnp.float32)),
        in_specs=[smem, anywhere, hbm, hbm],
        out_specs=(vmem, vmem, vmem),
        scratch_shapes=[pltpu.SemaphoreType.DMA((2,))],
        compiler_params=pltpu.CompilerParams(vmem_limit_bytes=8 * 2**20),
        cost_estimate=pl.CostEstimate(
            flops=0, bytes_accessed=3 * span * head_dim, transcendentals=0
        ),
    )(lengths, sent, in_hbm(k_cache.reshape(span, head_dim)), old_values)
    received = exchange(sent.reshape(rows, pieces, 1, head_dim), ("yh", "z", "x"))
    heads = 16
    attended = pl.pallas_call(
        attend,
        out_shape=jax.ShapeDtypeStruct((32, heads, head_dim), jnp.bfloat16),
        in_specs=[smem, vmem, vmem, vmem, vmem, hbm],
        out_specs=vmem,
        scratch_shapes=[
            pltpu.VMEM((heads, head_dim), jnp.float32),
            pltpu.VMEM((heads, span), jnp.float32),
            pltpu.VMEM((span, head_dim), v_cache.dtype),
            pltpu.SemaphoreType.DMA((2,)),
        ],
        compiler_params=pltpu.CompilerParams(vmem_limit_bytes=8 * 2**20),
    )(lengths, turns, received.reshape(-1, head_dim), keys, early, old_values)
    head_rows = w_out.shape[0]
    heads = head_rows // head_dim
    mine = exchange(attended.reshape(rows, heads, head_dim), SEQUENCES)
    out_terms = jnp.einsum(
        "shd,hdn->ns",
        mine,
        w_out.reshape(heads, head_dim, -1),
        preferred_element_type=jnp.float32,
    )
    out_parts = exchange(out_terms.reshape(16, -1, rows), HEADS)
    return jnp.sum(out_parts, axis=0).astype(jnp.bfloat16).T


def solution(mesh):
    split = Mesh(mesh.devices.reshape(8, 4, 2, 2, 4), ("z", "yh", "yl", "core", "x"))
    placed = (
        P(None, WIDTH + HEADS),
        P(WIDTH, HEADS),
        P(SEQUENCES, None, GROUPS, None),
        P(SEQUENCES, None, GROUPS, None),
        P(SEQUENCES),
        P(HEADS, WIDTH),
    )
    return jax.shard_map(
        shards, mesh=split, in_specs=placed, out_specs=P(None, WIDTH + HEADS), check_vma=False
    )
```

```python
import math

import jax
import jax.numpy as jnp
from jax import lax
from jax.experimental import pallas as pl
from jax.experimental.pallas import tpu as pltpu
from jax.sharding import Mesh
from jax.sharding import PartitionSpec as P

ROPE_BASE = 500000.0
LANES = 128
KEYS_STEP = 2048
EARLY = 4096
WIDTH = ("z", "yh")
GROUPS = ("yl", "core")
ACROSS = ("xa", "xb")
HEADS = GROUPS + ACROSS
SEQUENCES = WIDTH + ACROSS


def exchange(values, axes):
    return lax.all_to_all(values, axes, split_axis=0, concat_axis=0, tiled=True)


def load(values_ref, weights_ref, copies_ref, held_ref, first_ref, sems):
    weights = pltpu.make_async_copy(weights_ref, held_ref, sems.at[0])
    values = pltpu.make_async_copy(values_ref, first_ref, sems.at[1])
    values.start()
    weights.start()
    values.wait()
    copies_ref[...] = jnp.broadcast_to(first_ref[...][None], copies_ref.shape)
    weights.wait()


def in_hbm(values):
    return pltpu.with_memory_space_constraint(values, pltpu.HBM)


def fetch(
    length_ref,
    after_ref,
    keys_ref,
    values_ref,
    held_keys_ref,
    held_values_ref,
    turns_ref,
    sems,
):
    size = held_values_ref.shape[0]
    copies = [
        pltpu.make_async_copy(keys_ref, held_keys_ref, sems.at[0]),
        pltpu.make_async_copy(values_ref.at[pl.ds(0, size), :], held_values_ref, sems.at[1]),
    ]
    for copy in copies:
        copy.start()
    lane = lax.broadcasted_iota(jnp.int32, (8, LANES), 1)
    half = LANES // 2
    first = lane < half
    spot = jnp.where(first, lane, lane - half).astype(jnp.float32)
    freqs = jnp.exp(spot * (-2.0 * math.log(ROPE_BASE) / LANES))
    angles = length_ref[0].astype(jnp.float32) * freqs
    sine = jnp.sin(angles)
    turns_ref[0] = jnp.cos(angles)
    turns_ref[1] = jnp.where(first, -sine, sine)
    for copy in copies:
        copy.wait()


def project(mine_ref, weights_ref, out_ref, terms_ref):
    rows = mine_ref.shape[1]
    terms = lax.dot_general(
        mine_ref[...],
        weights_ref[...],
        (((0,), (0,)), ((), ())),
        preferred_element_type=jnp.float32,
    )
    pieces = terms.shape[1] // LANES
    for piece in range(pieces):
        terms_ref[pl.ds(piece * rows, rows), :] = terms[:, piece * LANES : (piece + 1) * LANES]
    deep, near = 8, 4
    wide = rows // deep
    for place in range(wide):
        first = (place // near) * deep * near + place % near
        for piece in range(pieces):
            out_ref[pl.ds(first * pieces + piece, deep, stride=near * pieces), :] = terms_ref[
                pl.ds(piece * rows + place, deep, stride=wide), :
            ]


def attend(
    length_ref,
    half_ref,
    turns_ref,
    received_ref,
    keys_ref,
    early_ref,
    values_ref,
    out_ref,
    queries_ref,
    scores_ref,
    held_ref,
    sems,
):
    early = early_ref.shape[0]
    late = values_ref.shape[0] - early
    copies = [
        pltpu.make_async_copy(
            values_ref.at[pl.ds(early, late), :], held_ref.at[pl.ds(early, late), :], sems.at[0]
        ),
        pltpu.make_async_copy(early_ref, held_ref.at[pl.ds(0, early), :], sems.at[1]),
    ]
    for copy in copies:
        copy.start()
    groups = 2
    length = length_ref[0]
    blocks = 4
    rows = received_ref.shape[0] // 32
    pieces = rows // blocks
    heads = pieces - 1
    sums = jnp.sum(received_ref[...].reshape(16, 2 * rows, LANES), axis=0)
    mixed = sums[:rows] + sums[rows:]
    mixed = mixed.astype(jnp.bfloat16).astype(jnp.float32)
    turned = mixed * turns_ref[0, :1] + pltpu.roll(mixed, LANES // 2, 1) * turns_ref[1, :1]
    turned = turned.astype(jnp.bfloat16).astype(jnp.float32)
    for block in range(blocks):
        queries_ref[pl.ds(block * heads, heads), :] = turned[
            block * pieces : block * pieces + heads
        ]
    queries = queries_ref[...]

    def new(values, block):
        return values[block * pieces + heads : (block + 1) * pieces]

    scale = 1.0 / math.sqrt(LANES)
    row_group = lax.broadcasted_iota(jnp.int32, (4 * heads, 1), 0) // (2 * heads)
    key_new = jnp.where(row_group == 0, new(turned, 0), new(turned, 2))
    value_new = jnp.where(row_group == 0, new(mixed, 1), new(mixed, 3))
    own = jnp.sum(queries * key_new, axis=1, keepdims=True) * scale
    queries = queries.astype(jnp.bfloat16)
    span = keys_ref.shape[0]
    steps = span // KEYS_STEP
    column = lax.broadcasted_iota(jnp.int32, (4 * heads, KEYS_STEP), 1)
    same = (column % groups) == row_group
    place = jnp.where(same, column, groups * span)
    top = own
    for step in range(steps):
        block = pl.ds(step * KEYS_STEP, KEYS_STEP)
        scores = lax.dot_general(
            queries,
            keys_ref[block, :],
            (((1,), (1,)), ((), ())),
            preferred_element_type=jnp.float32,
        ) * scale
        scores = jnp.where(place < groups * length - step * KEYS_STEP, scores, -jnp.inf)
        scores_ref[:, block] = scores
        top = jnp.maximum(top, jnp.max(scores, axis=1, keepdims=True))
    own = jnp.exp(own - top)
    total = own
    for step in range(steps):
        block = pl.ds(step * KEYS_STEP, KEYS_STEP)
        exponent = jnp.exp(scores_ref[:, block] - top)
        scores_ref[:, block] = exponent
        total = total + jnp.sum(exponent, axis=1, keepdims=True)
    inverse = 1.0 / total
    own = (own * inverse).astype(jnp.bfloat16).astype(jnp.float32)
    attended = own * value_new
    for copy in copies:
        copy.wait()
    for step in range(steps):
        block = pl.ds(step * KEYS_STEP, KEYS_STEP)
        weights = (scores_ref[:, block] * inverse).astype(jnp.bfloat16)
        attended = attended + jnp.dot(
            weights, held_ref[block, :], preferred_element_type=jnp.float32
        )
    size = attended.shape[0] // 4
    block = [attended[i * size : (i + 1) * size] for i in range(4)]
    lower = jnp.concatenate([block[0], block[3], block[1], block[2]], axis=0)
    upper = jnp.concatenate([block[2], block[1], block[3], block[0]], axis=0)
    ordered = jnp.where(half_ref[0] == 0, lower, upper).astype(jnp.bfloat16)
    out_ref[...] = jnp.broadcast_to(ordered[None], out_ref.shape)


def finish(half_ref, first_ref, received_ref, weights_ref, out_ref, rows_ref):
    heads = weights_ref.shape[0] // LANES
    count = first_ref.shape[0]
    rows_ref[...] = received_ref[...].astype(jnp.float32)
    ours = jnp.concatenate(
        [
            rows_ref[pl.ds(heads + head, count, stride=2 * heads), :]
            for head in range(heads)
        ],
        axis=1,
    ).astype(jnp.bfloat16)
    sequence = lax.broadcasted_iota(jnp.int32, (count, 2 * count), 1)
    source = lax.broadcasted_iota(jnp.int32, (count, 2 * count), 0)
    place = source + 2 * (source // 2) + 2 * half_ref[0]
    chosen = (sequence == place).astype(jnp.float32)
    terms = first_ref[...] + jnp.dot(
        ours, weights_ref[...], preferred_element_type=jnp.float32
    )
    out_ref[...] = lax.dot_general(
        terms,
        chosen,
        (((0,), (0,)), ((), ())),
        precision=lax.Precision.HIGHEST,
        preferred_element_type=jnp.float32,
    )


def shards(activations, w_qkv, k_cache, v_cache, lengths, w_out):
    out_cols = w_qkv.shape[1]
    head_dim = k_cache.shape[3]
    rows = activations.shape[0]
    vmem = pl.BlockSpec(memory_space=pltpu.VMEM)
    hbm = pl.BlockSpec(memory_space=pltpu.HBM)
    anywhere = pl.BlockSpec(memory_space=pl.ANY)
    pieces = out_cols // head_dim
    copies, weights = pl.pallas_call(
        load,
        out_shape=(
            jax.ShapeDtypeStruct((16,) + activations.T.shape, activations.dtype),
            jax.ShapeDtypeStruct(w_qkv.shape, w_qkv.dtype),
        ),
        in_specs=[hbm, hbm],
        out_specs=(vmem, vmem),
        scratch_shapes=[
            pltpu.VMEM(activations.T.shape, activations.dtype),
            pltpu.SemaphoreType.DMA((2,)),
        ],
        compiler_params=pltpu.CompilerParams(vmem_limit_bytes=4 * 2**20),
    )(in_hbm(activations.T), in_hbm(w_qkv))
    mine_t = exchange(copies, HEADS)
    sent = pl.pallas_call(
        project,
        out_shape=jax.ShapeDtypeStruct((rows * pieces, head_dim), jnp.float32),
        in_specs=[vmem, vmem],
        out_specs=vmem,
        scratch_shapes=[pltpu.VMEM((rows * pieces, head_dim), jnp.float32)],
        compiler_params=pltpu.CompilerParams(vmem_limit_bytes=4 * 2**20),
    )(mine_t.reshape(-1, rows), weights)
    span = k_cache.shape[1] * k_cache.shape[2]
    cache = jax.ShapeDtypeStruct((span, head_dim), k_cache.dtype)
    early_cache = jax.ShapeDtypeStruct((EARLY, head_dim), v_cache.dtype)
    old_values = in_hbm(v_cache.reshape(span, head_dim))
    smem = pl.BlockSpec(memory_space=pltpu.SMEM)
    keys, early, turns = pl.pallas_call(
        fetch,
        out_shape=(cache, early_cache, jax.ShapeDtypeStruct((2, 8, LANES), jnp.float32)),
        in_specs=[smem, anywhere, hbm, hbm],
        out_specs=(vmem, vmem, vmem),
        scratch_shapes=[pltpu.SemaphoreType.DMA((2,))],
        compiler_params=pltpu.CompilerParams(vmem_limit_bytes=8 * 2**20),
        cost_estimate=pl.CostEstimate(
            flops=0, bytes_accessed=3 * span * head_dim, transcendentals=0
        ),
    )(lengths, sent, in_hbm(k_cache.reshape(span, head_dim)), old_values)
    received = exchange(sent.reshape(rows, pieces, 1, head_dim), ("yh", "z") + ACROSS)
    w_late, _ = lax.optimization_barrier((w_out, sent))
    w_other = lax.ppermute(w_late, ACROSS, [(i, 3 - i) for i in range(4)])
    half = lax.axis_index("xa").reshape(1)
    heads = 16
    attended = pl.pallas_call(
        attend,
        out_shape=jax.ShapeDtypeStruct((32, heads, head_dim), jnp.bfloat16),
        in_specs=[smem, smem, vmem, vmem, vmem, vmem, hbm],
        out_specs=vmem,
        scratch_shapes=[
            pltpu.VMEM((heads, head_dim), jnp.float32),
            pltpu.VMEM((heads, span), jnp.float32),
            pltpu.VMEM((span, head_dim), v_cache.dtype),
            pltpu.SemaphoreType.DMA((2,)),
        ],
        compiler_params=pltpu.CompilerParams(vmem_limit_bytes=8 * 2**20),
    )(lengths, half, turns, received.reshape(-1, head_dim), keys, early, old_values)
    near = WIDTH + ("xb",)
    mine = exchange(attended.reshape(rows // 2, heads // 2, head_dim), near)
    own_terms = jnp.einsum(
        "shd,hdn->sn",
        mine[:, : heads // 4],
        w_out.reshape(heads // 4, head_dim, -1),
        preferred_element_type=jnp.float32,
    )
    out_terms = pl.pallas_call(
        finish,
        out_shape=jax.ShapeDtypeStruct((w_out.shape[1], rows), jnp.float32),
        in_specs=[smem, vmem, vmem, vmem],
        out_specs=vmem,
        scratch_shapes=[pltpu.VMEM((rows * 4, head_dim), jnp.float32)],
        compiler_params=pltpu.CompilerParams(vmem_limit_bytes=4 * 2**20),
    )(half, own_terms, mine.reshape(-1, head_dim), w_other)
    out_parts = exchange(out_terms.reshape(16, -1, rows), HEADS)
    return jnp.sum(out_parts, axis=0).astype(jnp.bfloat16).T


def solution(mesh):
    split = Mesh(
        mesh.devices.reshape(8, 4, 2, 2, 2, 2), ("z", "yh", "yl", "core", "xa", "xb")
    )
    placed = (
        P(None, WIDTH + HEADS),
        P(WIDTH, HEADS),
        P(SEQUENCES, None, GROUPS, None),
        P(SEQUENCES, None, GROUPS, None),
        P(SEQUENCES),
        P(HEADS, WIDTH),
    )
    return jax.shard_map(
        shards, mesh=split, in_specs=placed, out_specs=P(None, WIDTH + HEADS), check_vma=False
    )
```

```python
import math

import jax
import jax.numpy as jnp
from jax import lax
from jax.experimental import pallas as pl
from jax.experimental.pallas import tpu as pltpu
from jax.sharding import Mesh
from jax.sharding import PartitionSpec as P

ROPE_BASE = 500000.0
LANES = 128
KEYS_STEP = 2048
EARLY = 3072
WIDTH = ("z", "yh")
GROUPS = ("yl", "core")
ACROSS = ("xa", "xb")
HEADS = GROUPS + ACROSS
SEQUENCES = WIDTH + ACROSS


def exchange(values, axes):
    return lax.all_to_all(values, axes, split_axis=0, concat_axis=0, tiled=True)


def load(values_ref, weights_ref, copies_ref, held_ref, first_ref, sems):
    weights = pltpu.make_async_copy(weights_ref, held_ref, sems.at[0])
    values = pltpu.make_async_copy(values_ref, first_ref, sems.at[1])
    values.start()
    weights.start()
    values.wait()
    copies_ref[...] = jnp.broadcast_to(first_ref[...][None], copies_ref.shape)
    weights.wait()


def in_hbm(values):
    return pltpu.with_memory_space_constraint(values, pltpu.HBM)


def fetch(
    length_ref,
    after_ref,
    keys_ref,
    values_ref,
    held_keys_ref,
    held_values_ref,
    turns_ref,
    sems,
):
    size = held_values_ref.shape[0]
    copies = [
        pltpu.make_async_copy(keys_ref, held_keys_ref, sems.at[0]),
        pltpu.make_async_copy(values_ref.at[pl.ds(0, size), :], held_values_ref, sems.at[1]),
    ]
    for copy in copies:
        copy.start()
    lane = lax.broadcasted_iota(jnp.int32, (8, LANES), 1)
    half = LANES // 2
    first = lane < half
    spot = jnp.where(first, lane, lane - half).astype(jnp.float32)
    freqs = jnp.exp(spot * (-2.0 * math.log(ROPE_BASE) / LANES))
    angles = length_ref[0].astype(jnp.float32) * freqs
    sine = jnp.sin(angles)
    turns_ref[0] = jnp.cos(angles)
    turns_ref[1] = jnp.where(first, -sine, sine)
    for copy in copies:
        copy.wait()


def project(mine_ref, weights_ref, out_ref, terms_ref):
    rows = mine_ref.shape[1]
    terms = lax.dot_general(
        mine_ref[...],
        weights_ref[...],
        (((0,), (0,)), ((), ())),
        preferred_element_type=jnp.float32,
    )
    pieces = terms.shape[1] // LANES
    for piece in range(pieces):
        terms_ref[pl.ds(piece * rows, rows), :] = terms[:, piece * LANES : (piece + 1) * LANES]
    deep, near = 8, 4
    wide = rows // deep
    for place in range(wide):
        first = (place // near) * deep * near + place % near
        for piece in range(pieces):
            out_ref[pl.ds(first * pieces + piece, deep, stride=near * pieces), :] = terms_ref[
                pl.ds(piece * rows + place, deep, stride=wide), :
            ]


def attend(
    length_ref,
    half_ref,
    turns_ref,
    received_ref,
    keys_ref,
    early_ref,
    values_ref,
    out_ref,
    queries_ref,
    scores_ref,
    held_ref,
    sems,
):
    early = early_ref.shape[0]
    late = values_ref.shape[0] - early
    copies = [
        pltpu.make_async_copy(
            values_ref.at[pl.ds(early, late), :], held_ref.at[pl.ds(early, late), :], sems.at[0]
        ),
        pltpu.make_async_copy(early_ref, held_ref.at[pl.ds(0, early), :], sems.at[1]),
    ]
    for copy in copies:
        copy.start()
    groups = 2
    length = length_ref[0]
    blocks = 4
    rows = received_ref.shape[0] // 32
    pieces = rows // blocks
    heads = pieces - 1
    sums = jnp.sum(received_ref[...].reshape(16, 2 * rows, LANES), axis=0)
    mixed = sums[:rows] + sums[rows:]
    mixed = mixed.astype(jnp.bfloat16).astype(jnp.float32)
    turned = mixed * turns_ref[0, :1] + pltpu.roll(mixed, LANES // 2, 1) * turns_ref[1, :1]
    turned = turned.astype(jnp.bfloat16).astype(jnp.float32)
    for block in range(blocks):
        queries_ref[pl.ds(block * heads, heads), :] = turned[
            block * pieces : block * pieces + heads
        ]
    queries = queries_ref[...]

    def new(values, block):
        return values[block * pieces + heads : (block + 1) * pieces]

    scale = 1.0 / math.sqrt(LANES)
    row_group = lax.broadcasted_iota(jnp.int32, (4 * heads, 1), 0) // (2 * heads)
    key_new = jnp.where(row_group == 0, new(turned, 0), new(turned, 2))
    value_new = jnp.where(row_group == 0, new(mixed, 1), new(mixed, 3))
    own = jnp.sum(queries * key_new, axis=1, keepdims=True) * scale
    queries = queries.astype(jnp.bfloat16)
    span = keys_ref.shape[0]
    steps = span // KEYS_STEP
    column = lax.broadcasted_iota(jnp.int32, (4 * heads, KEYS_STEP), 1)
    same = (column % groups) == row_group
    place = jnp.where(same, column, groups * span)
    top = own
    for step in range(steps):
        block = pl.ds(step * KEYS_STEP, KEYS_STEP)
        scores = lax.dot_general(
            queries,
            keys_ref[block, :],
            (((1,), (1,)), ((), ())),
            preferred_element_type=jnp.float32,
        ) * scale
        scores = jnp.where(place < groups * length - step * KEYS_STEP, scores, -jnp.inf)
        scores_ref[:, block] = scores
        top = jnp.maximum(top, jnp.max(scores, axis=1, keepdims=True))
    own = jnp.exp(own - top)
    total = own
    for step in range(steps):
        block = pl.ds(step * KEYS_STEP, KEYS_STEP)
        exponent = jnp.exp(scores_ref[:, block] - top)
        scores_ref[:, block] = exponent
        total = total + jnp.sum(exponent, axis=1, keepdims=True)
    inverse = 1.0 / total
    own = (own * inverse).astype(jnp.bfloat16).astype(jnp.float32)
    attended = own * value_new
    for copy in copies:
        copy.wait()
    for step in range(steps):
        block = pl.ds(step * KEYS_STEP, KEYS_STEP)
        weights = (scores_ref[:, block] * inverse).astype(jnp.bfloat16)
        attended = attended + jnp.dot(
            weights, held_ref[block, :], preferred_element_type=jnp.float32
        )
    size = attended.shape[0] // 4
    block = [attended[i * size : (i + 1) * size] for i in range(4)]
    lower = jnp.concatenate([block[0], block[3], block[1], block[2]], axis=0)
    upper = jnp.concatenate([block[2], block[1], block[3], block[0]], axis=0)
    ordered = jnp.where(half_ref[0] == 0, lower, upper).astype(jnp.bfloat16)
    out_ref[...] = jnp.broadcast_to(ordered[None], out_ref.shape)


def finish(half_ref, first_ref, received_ref, weights_ref, out_ref, rows_ref):
    heads = weights_ref.shape[0] // LANES
    count = first_ref.shape[0]
    rows_ref[...] = received_ref[...].astype(jnp.float32)
    ours = jnp.concatenate(
        [
            rows_ref[pl.ds(heads + head, count, stride=2 * heads), :]
            for head in range(heads)
        ],
        axis=1,
    ).astype(jnp.bfloat16)
    sequence = lax.broadcasted_iota(jnp.int32, (count, 2 * count), 1)
    source = lax.broadcasted_iota(jnp.int32, (count, 2 * count), 0)
    place = source + 2 * (source // 2) + 2 * half_ref[0]
    chosen = (sequence == place).astype(jnp.float32)
    terms = first_ref[...] + jnp.dot(
        ours, weights_ref[...], preferred_element_type=jnp.float32
    )
    out_ref[...] = lax.dot_general(
        terms,
        chosen,
        (((0,), (0,)), ((), ())),
        precision=lax.Precision.HIGHEST,
        preferred_element_type=jnp.float32,
    )


def shards(activations, w_qkv, k_cache, v_cache, lengths, w_out):
    out_cols = w_qkv.shape[1]
    head_dim = k_cache.shape[3]
    rows = activations.shape[0]
    vmem = pl.BlockSpec(memory_space=pltpu.VMEM)
    hbm = pl.BlockSpec(memory_space=pltpu.HBM)
    anywhere = pl.BlockSpec(memory_space=pl.ANY)
    pieces = out_cols // head_dim
    copies, weights = pl.pallas_call(
        load,
        out_shape=(
            jax.ShapeDtypeStruct((16,) + activations.T.shape, activations.dtype),
            jax.ShapeDtypeStruct(w_qkv.shape, w_qkv.dtype),
        ),
        in_specs=[hbm, hbm],
        out_specs=(vmem, vmem),
        scratch_shapes=[
            pltpu.VMEM(activations.T.shape, activations.dtype),
            pltpu.SemaphoreType.DMA((2,)),
        ],
        compiler_params=pltpu.CompilerParams(vmem_limit_bytes=4 * 2**20),
    )(in_hbm(activations.T), in_hbm(w_qkv))
    mine_t = exchange(copies, HEADS)
    sent = pl.pallas_call(
        project,
        out_shape=jax.ShapeDtypeStruct((rows * pieces, head_dim), jnp.float32),
        in_specs=[vmem, vmem],
        out_specs=vmem,
        scratch_shapes=[pltpu.VMEM((rows * pieces, head_dim), jnp.float32)],
        compiler_params=pltpu.CompilerParams(vmem_limit_bytes=4 * 2**20),
    )(mine_t.reshape(-1, rows), weights)
    span = k_cache.shape[1] * k_cache.shape[2]
    cache = jax.ShapeDtypeStruct((span, head_dim), k_cache.dtype)
    early_cache = jax.ShapeDtypeStruct((EARLY, head_dim), v_cache.dtype)
    old_values = in_hbm(v_cache.reshape(span, head_dim))
    smem = pl.BlockSpec(memory_space=pltpu.SMEM)
    keys, early, turns = pl.pallas_call(
        fetch,
        out_shape=(cache, early_cache, jax.ShapeDtypeStruct((2, 8, LANES), jnp.float32)),
        in_specs=[smem, anywhere, hbm, hbm],
        out_specs=(vmem, vmem, vmem),
        scratch_shapes=[pltpu.SemaphoreType.DMA((2,))],
        compiler_params=pltpu.CompilerParams(vmem_limit_bytes=8 * 2**20),
        cost_estimate=pl.CostEstimate(
            flops=0, bytes_accessed=3 * span * head_dim, transcendentals=0
        ),
    )(lengths, sent, in_hbm(k_cache.reshape(span, head_dim)), old_values)
    received = exchange(sent.reshape(rows, pieces, 1, head_dim), ("yh", "z") + ACROSS)
    w_late, _ = lax.optimization_barrier((w_out, sent))
    w_other = lax.ppermute(w_late, ACROSS, [(i, 3 - i) for i in range(4)])
    half = lax.axis_index("xa").reshape(1)
    heads = 16
    attended = pl.pallas_call(
        attend,
        out_shape=jax.ShapeDtypeStruct((32, heads, head_dim), jnp.bfloat16),
        in_specs=[smem, smem, vmem, vmem, vmem, vmem, hbm],
        out_specs=vmem,
        scratch_shapes=[
            pltpu.VMEM((heads, head_dim), jnp.float32),
            pltpu.VMEM((heads, span), jnp.float32),
            pltpu.VMEM((span, head_dim), v_cache.dtype),
            pltpu.SemaphoreType.DMA((2,)),
        ],
        compiler_params=pltpu.CompilerParams(vmem_limit_bytes=8 * 2**20),
    )(lengths, half, turns, received.reshape(-1, head_dim), keys, early, old_values)
    near = WIDTH + ("xb",)
    mine = exchange(attended.reshape(rows // 2, heads // 2, head_dim), near)
    own_terms = jnp.einsum(
        "shd,hdn->sn",
        mine[:, : heads // 4],
        w_out.reshape(heads // 4, head_dim, -1),
        preferred_element_type=jnp.float32,
    )
    out_terms = pl.pallas_call(
        finish,
        out_shape=jax.ShapeDtypeStruct((w_out.shape[1], rows), jnp.float32),
        in_specs=[smem, vmem, vmem, vmem],
        out_specs=vmem,
        scratch_shapes=[pltpu.VMEM((rows * 4, head_dim), jnp.float32)],
        compiler_params=pltpu.CompilerParams(vmem_limit_bytes=4 * 2**20),
    )(half, own_terms, mine.reshape(-1, head_dim), w_other)
    out_parts = exchange(out_terms.reshape(16, -1, rows), HEADS)
    return jnp.sum(out_parts, axis=0).astype(jnp.bfloat16).T


def solution(mesh):
    split = Mesh(
        mesh.devices.reshape(8, 4, 2, 2, 2, 2), ("z", "yh", "yl", "core", "xa", "xb")
    )
    placed = (
        P(None, WIDTH + HEADS),
        P(WIDTH, HEADS),
        P(SEQUENCES, None, GROUPS, None),
        P(SEQUENCES, None, GROUPS, None),
        P(SEQUENCES),
        P(HEADS, WIDTH),
    )
    return jax.shard_map(
        shards, mesh=split, in_specs=placed, out_specs=P(None, WIDTH + HEADS), check_vma=False
    )
```

```python
import math

import jax
import jax.numpy as jnp
from jax import lax
from jax.experimental import pallas as pl
from jax.experimental.pallas import tpu as pltpu
from jax.sharding import Mesh
from jax.sharding import PartitionSpec as P

ROPE_BASE = 500000.0
LANES = 128
KEYS_STEP = 2048
EARLY = 3072
SCALE = 64.0
WIDTH = ("z", "yh")
GROUPS = ("yl", "core")
ACROSS = ("xa", "xb")
HEADS = GROUPS + ACROSS
SEQUENCES = WIDTH + ACROSS


def exchange(values, axes):
    return lax.all_to_all(values, axes, split_axis=0, concat_axis=0, tiled=True)


def load(values_ref, weights_ref, copies_ref, held_ref, first_ref, sems):
    weights = pltpu.make_async_copy(weights_ref, held_ref, sems.at[0])
    values = pltpu.make_async_copy(values_ref, first_ref, sems.at[1])
    values.start()
    weights.start()
    values.wait()
    copies_ref[...] = jnp.broadcast_to(first_ref[...][None], copies_ref.shape)
    weights.wait()


def in_hbm(values):
    return pltpu.with_memory_space_constraint(values, pltpu.HBM)


def fetch(
    length_ref,
    after_ref,
    keys_ref,
    values_ref,
    held_keys_ref,
    held_values_ref,
    turns_ref,
    sems,
):
    size = held_values_ref.shape[0]
    copies = [
        pltpu.make_async_copy(keys_ref, held_keys_ref, sems.at[0]),
        pltpu.make_async_copy(values_ref.at[pl.ds(0, size), :], held_values_ref, sems.at[1]),
    ]
    for copy in copies:
        copy.start()
    lane = lax.broadcasted_iota(jnp.int32, (8, LANES), 1)
    half = LANES // 2
    first = lane < half
    spot = jnp.where(first, lane, lane - half).astype(jnp.float32)
    freqs = jnp.exp(spot * (-2.0 * math.log(ROPE_BASE) / LANES))
    angles = length_ref[0].astype(jnp.float32) * freqs
    sine = jnp.sin(angles)
    turns_ref[0] = jnp.cos(angles)
    turns_ref[1] = jnp.where(first, -sine, sine)
    for copy in copies:
        copy.wait()


def project(mine_ref, weights_ref, out_ref, terms_ref):
    rows = mine_ref.shape[1]
    terms = lax.dot_general(
        mine_ref[...],
        weights_ref[...],
        (((0,), (0,)), ((), ())),
        preferred_element_type=jnp.float32,
    )
    pieces = terms.shape[1] // LANES
    for piece in range(pieces):
        terms_ref[pl.ds(piece * rows, rows), :] = terms[:, piece * LANES : (piece + 1) * LANES]
    held = out_ref.shape[0] // rows
    deep, near = 8, 4
    wide = rows // deep
    for place in range(wide):
        first = (place // near) * deep * near + place % near
        for piece in range(pieces):
            out_ref[pl.ds(first * held + piece, deep, stride=near * held), :] = terms_ref[
                pl.ds(piece * rows + place, deep, stride=wide), :
            ]
    for piece in range(pieces, held):
        out_ref[pl.ds(piece, rows, stride=held), :] = jnp.zeros((rows, LANES), jnp.float32)


def attend(
    length_ref,
    half_ref,
    turns_ref,
    received_ref,
    keys_ref,
    early_ref,
    values_ref,
    out_ref,
    queries_ref,
    scores_ref,
    held_ref,
    sems,
):
    early = early_ref.shape[0]
    late = values_ref.shape[0] - early
    copies = [
        pltpu.make_async_copy(
            values_ref.at[pl.ds(early, late), :], held_ref.at[pl.ds(early, late), :], sems.at[0]
        ),
        pltpu.make_async_copy(early_ref, held_ref.at[pl.ds(0, early), :], sems.at[1]),
    ]
    for copy in copies:
        copy.start()
    groups = 2
    length = length_ref[0]
    blocks = 4
    rows = received_ref.shape[0] // 32
    pieces = rows // blocks
    heads = pieces - 2
    mixed = jnp.sum(received_ref[...].reshape(32, rows, LANES), axis=0) * (1.0 / SCALE)
    mixed = mixed.astype(jnp.bfloat16).astype(jnp.float32)
    turned = mixed * turns_ref[0, :1] + pltpu.roll(mixed, LANES // 2, 1) * turns_ref[1, :1]
    turned = turned.astype(jnp.bfloat16).astype(jnp.float32)
    for block in range(blocks):
        queries_ref[pl.ds(block * heads, heads), :] = turned[
            block * pieces : block * pieces + heads
        ]
    queries = queries_ref[...]

    def new(values, block):
        return values[block * pieces + heads : block * pieces + heads + 1]

    scale = 1.0 / math.sqrt(LANES)
    row_group = lax.broadcasted_iota(jnp.int32, (4 * heads, 1), 0) // (2 * heads)
    key_new = jnp.where(row_group == 0, new(turned, 0), new(turned, 2))
    value_new = jnp.where(row_group == 0, new(mixed, 1), new(mixed, 3))
    own = jnp.sum(queries * key_new, axis=1, keepdims=True) * scale
    queries = queries.astype(jnp.bfloat16)
    span = keys_ref.shape[0]
    steps = span // KEYS_STEP
    column = lax.broadcasted_iota(jnp.int32, (4 * heads, KEYS_STEP), 1)
    same = (column % groups) == row_group
    place = jnp.where(same, column, groups * span)
    top = own
    for step in range(steps):
        block = pl.ds(step * KEYS_STEP, KEYS_STEP)
        scores = lax.dot_general(
            queries,
            keys_ref[block, :],
            (((1,), (1,)), ((), ())),
            preferred_element_type=jnp.float32,
        ) * scale
        scores = jnp.where(place < groups * length - step * KEYS_STEP, scores, -jnp.inf)
        scores_ref[:, block] = scores
        top = jnp.maximum(top, jnp.max(scores, axis=1, keepdims=True))
    own = jnp.exp(own - top)
    total = own
    for step in range(steps):
        block = pl.ds(step * KEYS_STEP, KEYS_STEP)
        exponent = jnp.exp(scores_ref[:, block] - top)
        scores_ref[:, block] = exponent
        total = total + jnp.sum(exponent, axis=1, keepdims=True)
    inverse = 1.0 / total
    own = (own * inverse).astype(jnp.bfloat16).astype(jnp.float32)
    attended = own * value_new
    for copy in copies:
        copy.wait()
    for step in range(steps):
        block = pl.ds(step * KEYS_STEP, KEYS_STEP)
        weights = (scores_ref[:, block] * inverse).astype(jnp.bfloat16)
        attended = attended + jnp.dot(
            weights, held_ref[block, :], preferred_element_type=jnp.float32
        )
    size = attended.shape[0] // 4
    block = [attended[i * size : (i + 1) * size] for i in range(4)]
    lower = jnp.concatenate([block[0], block[3], block[1], block[2]], axis=0)
    upper = jnp.concatenate([block[2], block[1], block[3], block[0]], axis=0)
    ordered = jnp.where(half_ref[0] == 0, lower, upper).astype(jnp.bfloat16)
    out_ref[...] = jnp.broadcast_to(ordered[None], out_ref.shape)


def finish(half_ref, first_ref, received_ref, weights_ref, out_ref, rows_ref):
    heads = weights_ref.shape[0] // LANES
    count = first_ref.shape[0]
    rows_ref[...] = received_ref[...].astype(jnp.float32)
    ours = jnp.concatenate(
        [
            rows_ref[pl.ds(heads + head, count, stride=2 * heads), :]
            for head in range(heads)
        ],
        axis=1,
    ).astype(jnp.bfloat16)
    sequence = lax.broadcasted_iota(jnp.int32, (count, 2 * count), 1)
    source = lax.broadcasted_iota(jnp.int32, (count, 2 * count), 0)
    place = source + 2 * (source // 2) + 2 * half_ref[0]
    chosen = (sequence == place).astype(jnp.float32)
    terms = first_ref[...] + jnp.dot(
        ours, weights_ref[...], preferred_element_type=jnp.float32
    )
    out_ref[...] = lax.dot_general(
        terms,
        chosen,
        (((0,), (0,)), ((), ())),
        precision=lax.Precision.HIGHEST,
        preferred_element_type=jnp.float32,
    )


def shards(activations, w_qkv, k_cache, v_cache, lengths, w_out):
    out_cols = w_qkv.shape[1]
    head_dim = k_cache.shape[3]
    rows = activations.shape[0]
    vmem = pl.BlockSpec(memory_space=pltpu.VMEM)
    hbm = pl.BlockSpec(memory_space=pltpu.HBM)
    anywhere = pl.BlockSpec(memory_space=pl.ANY)
    pieces = out_cols // head_dim
    pairs = (pieces + 1) // 2
    copies, weights = pl.pallas_call(
        load,
        out_shape=(
            jax.ShapeDtypeStruct((16,) + activations.T.shape, activations.dtype),
            jax.ShapeDtypeStruct(w_qkv.shape, w_qkv.dtype),
        ),
        in_specs=[hbm, hbm],
        out_specs=(vmem, vmem),
        scratch_shapes=[
            pltpu.VMEM(activations.T.shape, activations.dtype),
            pltpu.SemaphoreType.DMA((2,)),
        ],
        compiler_params=pltpu.CompilerParams(vmem_limit_bytes=4 * 2**20),
    )(in_hbm(activations.T), in_hbm(w_qkv))
    mine_t = exchange(copies, HEADS)
    sent = pl.pallas_call(
        project,
        out_shape=jax.ShapeDtypeStruct((rows * 2 * pairs, head_dim), jnp.float32),
        in_specs=[vmem, vmem],
        out_specs=vmem,
        scratch_shapes=[
            pltpu.VMEM((rows * pieces, head_dim), jnp.float32),
        ],
        compiler_params=pltpu.CompilerParams(vmem_limit_bytes=4 * 2**20),
    )(mine_t.reshape(-1, rows), weights)
    halves = (sent * SCALE).astype(jnp.float16)
    span = k_cache.shape[1] * k_cache.shape[2]
    cache = jax.ShapeDtypeStruct((span, head_dim), k_cache.dtype)
    early_cache = jax.ShapeDtypeStruct((EARLY, head_dim), v_cache.dtype)
    old_values = in_hbm(v_cache.reshape(span, head_dim))
    smem = pl.BlockSpec(memory_space=pltpu.SMEM)
    keys, early, turns = pl.pallas_call(
        fetch,
        out_shape=(cache, early_cache, jax.ShapeDtypeStruct((2, 8, LANES), jnp.float32)),
        in_specs=[smem, anywhere, hbm, hbm],
        out_specs=(vmem, vmem, vmem),
        scratch_shapes=[pltpu.SemaphoreType.DMA((2,))],
        compiler_params=pltpu.CompilerParams(vmem_limit_bytes=8 * 2**20),
        cost_estimate=pl.CostEstimate(
            flops=0, bytes_accessed=3 * span * head_dim, transcendentals=0
        ),
    )(lengths, sent, in_hbm(k_cache.reshape(span, head_dim)), old_values)
    received = exchange(halves.reshape(rows, pairs, 2, head_dim), ("yh", "z") + ACROSS)
    w_late, _ = lax.optimization_barrier((w_out, sent))
    w_other = lax.ppermute(w_late, ACROSS, [(i, 3 - i) for i in range(4)])
    half = lax.axis_index("xa").reshape(1)
    heads = 16
    attended = pl.pallas_call(
        attend,
        out_shape=jax.ShapeDtypeStruct((32, heads, head_dim), jnp.bfloat16),
        in_specs=[smem, smem, vmem, vmem, vmem, vmem, hbm],
        out_specs=vmem,
        scratch_shapes=[
            pltpu.VMEM((heads, head_dim), jnp.float32),
            pltpu.VMEM((heads, span), jnp.float32),
            pltpu.VMEM((span, head_dim), v_cache.dtype),
            pltpu.SemaphoreType.DMA((2,)),
        ],
        compiler_params=pltpu.CompilerParams(vmem_limit_bytes=8 * 2**20),
    )(lengths, half, turns, received.astype(jnp.float32).reshape(-1, head_dim), keys, early, old_values)
    near = WIDTH + ("xb",)
    mine = exchange(attended.reshape(rows // 2, heads // 2, head_dim), near)
    own_terms = jnp.einsum(
        "shd,hdn->sn",
        mine[:, : heads // 4],
        w_out.reshape(heads // 4, head_dim, -1),
        preferred_element_type=jnp.float32,
    )
    out_terms = pl.pallas_call(
        finish,
        out_shape=jax.ShapeDtypeStruct((w_out.shape[1], rows), jnp.float32),
        in_specs=[smem, vmem, vmem, vmem],
        out_specs=vmem,
        scratch_shapes=[pltpu.VMEM((rows * 4, head_dim), jnp.float32)],
        compiler_params=pltpu.CompilerParams(vmem_limit_bytes=4 * 2**20),
    )(half, own_terms, mine.reshape(-1, head_dim), w_other)
    out_parts = exchange(out_terms.reshape(16, -1, rows), HEADS)
    return jnp.sum(out_parts, axis=0).astype(jnp.bfloat16).T


def solution(mesh):
    split = Mesh(
        mesh.devices.reshape(8, 4, 2, 2, 2, 2), ("z", "yh", "yl", "core", "xa", "xb")
    )
    placed = (
        P(None, WIDTH + HEADS),
        P(WIDTH, HEADS),
        P(SEQUENCES, None, GROUPS, None),
        P(SEQUENCES, None, GROUPS, None),
        P(SEQUENCES),
        P(HEADS, WIDTH),
    )
    return jax.shard_map(
        shards, mesh=split, in_specs=placed, out_specs=P(None, WIDTH + HEADS), check_vma=False
    )
```

```python
import math

import jax
import jax.numpy as jnp
from jax import lax
from jax.experimental import pallas as pl
from jax.experimental.pallas import tpu as pltpu
from jax.sharding import Mesh
from jax.sharding import PartitionSpec as P

ROPE_BASE = 500000.0
LANES = 128
KEYS_STEP = 2048
EARLY = 3072
WIDTH = ("z", "yh")
GROUPS = ("yl", "core")
ACROSS = ("xa", "xb")
HEADS = GROUPS + ACROSS
SEQUENCES = WIDTH + ACROSS


def exchange(values, axes):
    return lax.all_to_all(values, axes, split_axis=0, concat_axis=0, tiled=True)


def load(values_ref, weights_ref, copies_ref, held_ref, first_ref, sems):
    weights = pltpu.make_async_copy(weights_ref, held_ref, sems.at[0])
    values = pltpu.make_async_copy(values_ref, first_ref, sems.at[1])
    values.start()
    weights.start()
    values.wait()
    copies_ref[...] = jnp.broadcast_to(first_ref[...][None], copies_ref.shape)
    weights.wait()


def in_hbm(values):
    return pltpu.with_memory_space_constraint(values, pltpu.HBM)


def fetch(
    length_ref,
    after_ref,
    keys_ref,
    values_ref,
    held_keys_ref,
    held_values_ref,
    turns_ref,
    sems,
):
    size = held_values_ref.shape[0]
    copies = [
        pltpu.make_async_copy(keys_ref, held_keys_ref, sems.at[0]),
        pltpu.make_async_copy(values_ref.at[pl.ds(0, size), :], held_values_ref, sems.at[1]),
    ]
    for copy in copies:
        copy.start()
    lane = lax.broadcasted_iota(jnp.int32, (8, LANES), 1)
    half = LANES // 2
    first = lane < half
    spot = jnp.where(first, lane, lane - half).astype(jnp.float32)
    freqs = jnp.exp(spot * (-2.0 * math.log(ROPE_BASE) / LANES))
    angles = length_ref[0].astype(jnp.float32) * freqs
    sine = jnp.sin(angles)
    turns_ref[0] = jnp.cos(angles)
    turns_ref[1] = jnp.where(first, -sine, sine)
    for copy in copies:
        copy.wait()


def project(mine_ref, weights_ref, out_ref, terms_ref):
    rows = mine_ref.shape[1]
    terms = lax.dot_general(
        mine_ref[...],
        weights_ref[...],
        (((0,), (0,)), ((), ())),
        preferred_element_type=jnp.float32,
    )
    pieces = terms.shape[1] // LANES
    for piece in range(pieces):
        terms_ref[pl.ds(piece * rows, rows), :] = terms[:, piece * LANES : (piece + 1) * LANES]
    deep, near = 8, 4
    wide = rows // deep
    for place in range(wide):
        first = (place // near) * deep * near + place % near
        for piece in range(pieces):
            out_ref[pl.ds(first * pieces + piece, deep, stride=near * pieces), :] = terms_ref[
                pl.ds(piece * rows + place, deep, stride=wide), :
            ]


def attend(
    length_ref,
    half_ref,
    turns_ref,
    received_ref,
    keys_ref,
    early_ref,
    values_ref,
    out_ref,
    queries_ref,
    scores_ref,
    held_ref,
    sems,
):
    early = early_ref.shape[0]
    late = values_ref.shape[0] - early
    copies = [
        pltpu.make_async_copy(
            values_ref.at[pl.ds(early, late), :], held_ref.at[pl.ds(early, late), :], sems.at[0]
        ),
        pltpu.make_async_copy(early_ref, held_ref.at[pl.ds(0, early), :], sems.at[1]),
    ]
    for copy in copies:
        copy.start()
    groups = 2
    length = length_ref[0]
    blocks = 4
    rows = received_ref.shape[0] // 32
    pieces = rows // blocks
    heads = pieces - 1
    sums = jnp.sum(received_ref[...].reshape(16, 2 * rows, LANES), axis=0)
    mixed = sums[:rows] + sums[rows:]
    mixed = mixed.astype(jnp.bfloat16).astype(jnp.float32)
    turned = mixed * turns_ref[0, :1] + pltpu.roll(mixed, LANES // 2, 1) * turns_ref[1, :1]
    turned = turned.astype(jnp.bfloat16).astype(jnp.float32)
    for block in range(blocks):
        queries_ref[pl.ds(block * heads, heads), :] = turned[
            block * pieces : block * pieces + heads
        ]
    queries = queries_ref[...]

    def new(values, block):
        return values[block * pieces + heads : (block + 1) * pieces]

    scale = 1.0 / math.sqrt(LANES)
    row_group = lax.broadcasted_iota(jnp.int32, (4 * heads, 1), 0) // (2 * heads)
    key_new = jnp.where(row_group == 0, new(turned, 0), new(turned, 2))
    value_new = jnp.where(row_group == 0, new(mixed, 1), new(mixed, 3))
    own = jnp.sum(queries * key_new, axis=1, keepdims=True) * scale
    queries = queries.astype(jnp.bfloat16)
    span = keys_ref.shape[0]
    steps = span // KEYS_STEP
    column = lax.broadcasted_iota(jnp.int32, (4 * heads, KEYS_STEP), 1)
    same = (column % groups) == row_group
    place = jnp.where(same, column, groups * span)
    top = own
    for step in range(steps):
        block = pl.ds(step * KEYS_STEP, KEYS_STEP)
        scores = lax.dot_general(
            queries,
            keys_ref[block, :],
            (((1,), (1,)), ((), ())),
            preferred_element_type=jnp.float32,
        ) * scale
        scores = jnp.where(place < groups * length - step * KEYS_STEP, scores, -jnp.inf)
        scores_ref[:, block] = scores
        top = jnp.maximum(top, jnp.max(scores, axis=1, keepdims=True))
    own = jnp.exp(own - top)
    total = own
    for step in range(steps):
        block = pl.ds(step * KEYS_STEP, KEYS_STEP)
        exponent = jnp.exp(scores_ref[:, block] - top)
        scores_ref[:, block] = exponent
        total = total + jnp.sum(exponent, axis=1, keepdims=True)
    inverse = 1.0 / total
    own = (own * inverse).astype(jnp.bfloat16).astype(jnp.float32)
    attended = own * value_new
    for copy in copies:
        copy.wait()
    for step in range(steps):
        block = pl.ds(step * KEYS_STEP, KEYS_STEP)
        weights = (scores_ref[:, block] * inverse).astype(jnp.bfloat16)
        attended = attended + jnp.dot(
            weights, held_ref[block, :], preferred_element_type=jnp.float32
        )
    size = attended.shape[0] // 4
    block = [attended[i * size : (i + 1) * size] for i in range(4)]
    lower = jnp.concatenate([block[0], block[3], block[1], block[2]], axis=0)
    upper = jnp.concatenate([block[2], block[1], block[3], block[0]], axis=0)
    ordered = jnp.where(half_ref[0] == 0, lower, upper).astype(jnp.bfloat16)
    out_ref[...] = jnp.broadcast_to(ordered[None], out_ref.shape)


def finish(half_ref, first_ref, received_ref, weights_ref, out_ref, rows_ref):
    heads = weights_ref.shape[0] // LANES
    count = first_ref.shape[0]
    rows_ref[...] = received_ref[...].astype(jnp.float32)
    ours = jnp.concatenate(
        [
            rows_ref[pl.ds(heads + head, count, stride=2 * heads), :]
            for head in range(heads)
        ],
        axis=1,
    ).astype(jnp.bfloat16)
    sequence = lax.broadcasted_iota(jnp.int32, (count, 2 * count), 1)
    source = lax.broadcasted_iota(jnp.int32, (count, 2 * count), 0)
    place = source + 2 * (source // 2) + 2 * half_ref[0]
    chosen = (sequence == place).astype(jnp.float32).astype(jnp.bfloat16)
    terms = first_ref[...] + jnp.dot(
        ours, weights_ref[...], preferred_element_type=jnp.float32
    )
    out_ref[...] = lax.dot_general(
        terms.astype(jnp.bfloat16),
        chosen,
        (((0,), (0,)), ((), ())),
        preferred_element_type=jnp.float32,
    ).astype(jnp.bfloat16)


def shards(activations, w_qkv, k_cache, v_cache, lengths, w_out):
    out_cols = w_qkv.shape[1]
    head_dim = k_cache.shape[3]
    rows = activations.shape[0]
    vmem = pl.BlockSpec(memory_space=pltpu.VMEM)
    hbm = pl.BlockSpec(memory_space=pltpu.HBM)
    anywhere = pl.BlockSpec(memory_space=pl.ANY)
    pieces = out_cols // head_dim
    copies, weights = pl.pallas_call(
        load,
        out_shape=(
            jax.ShapeDtypeStruct((16,) + activations.T.shape, activations.dtype),
            jax.ShapeDtypeStruct(w_qkv.shape, w_qkv.dtype),
        ),
        in_specs=[hbm, hbm],
        out_specs=(vmem, vmem),
        scratch_shapes=[
            pltpu.VMEM(activations.T.shape, activations.dtype),
            pltpu.SemaphoreType.DMA((2,)),
        ],
        compiler_params=pltpu.CompilerParams(vmem_limit_bytes=4 * 2**20),
    )(in_hbm(activations.T), in_hbm(w_qkv))
    mine_t = exchange(copies, HEADS)
    sent = pl.pallas_call(
        project,
        out_shape=jax.ShapeDtypeStruct((rows * pieces, head_dim), jnp.float32),
        in_specs=[vmem, vmem],
        out_specs=vmem,
        scratch_shapes=[pltpu.VMEM((rows * pieces, head_dim), jnp.float32)],
        compiler_params=pltpu.CompilerParams(vmem_limit_bytes=4 * 2**20),
    )(mine_t.reshape(-1, rows), weights)
    span = k_cache.shape[1] * k_cache.shape[2]
    cache = jax.ShapeDtypeStruct((span, head_dim), k_cache.dtype)
    early_cache = jax.ShapeDtypeStruct((EARLY, head_dim), v_cache.dtype)
    old_values = in_hbm(v_cache.reshape(span, head_dim))
    smem = pl.BlockSpec(memory_space=pltpu.SMEM)
    keys, early, turns = pl.pallas_call(
        fetch,
        out_shape=(cache, early_cache, jax.ShapeDtypeStruct((2, 8, LANES), jnp.float32)),
        in_specs=[smem, anywhere, hbm, hbm],
        out_specs=(vmem, vmem, vmem),
        scratch_shapes=[pltpu.SemaphoreType.DMA((2,))],
        compiler_params=pltpu.CompilerParams(vmem_limit_bytes=8 * 2**20),
        cost_estimate=pl.CostEstimate(
            flops=0, bytes_accessed=3 * span * head_dim, transcendentals=0
        ),
    )(lengths, sent, in_hbm(k_cache.reshape(span, head_dim)), old_values)
    received = exchange(sent.reshape(rows, pieces, 1, head_dim), ("yh", "z") + ACROSS)
    w_late, _ = lax.optimization_barrier((w_out, sent))
    w_other = lax.ppermute(w_late, ACROSS, [(i, 3 - i) for i in range(4)])
    half = lax.axis_index("xa").reshape(1)
    heads = 16
    attended = pl.pallas_call(
        attend,
        out_shape=jax.ShapeDtypeStruct((32, heads, head_dim), jnp.bfloat16),
        in_specs=[smem, smem, vmem, vmem, vmem, vmem, hbm],
        out_specs=vmem,
        scratch_shapes=[
            pltpu.VMEM((heads, head_dim), jnp.float32),
            pltpu.VMEM((heads, span), jnp.float32),
            pltpu.VMEM((span, head_dim), v_cache.dtype),
            pltpu.SemaphoreType.DMA((2,)),
        ],
        compiler_params=pltpu.CompilerParams(vmem_limit_bytes=8 * 2**20),
    )(lengths, half, turns, received.reshape(-1, head_dim), keys, early, old_values)
    near = WIDTH + ("xb",)
    mine = exchange(attended.reshape(rows // 2, heads // 2, head_dim), near)
    own_terms = jnp.einsum(
        "shd,hdn->sn",
        mine[:, : heads // 4],
        w_out.reshape(heads // 4, head_dim, -1),
        preferred_element_type=jnp.float32,
    )
    out_terms = pl.pallas_call(
        finish,
        out_shape=jax.ShapeDtypeStruct((w_out.shape[1], rows), jnp.bfloat16),
        in_specs=[smem, vmem, vmem, vmem],
        out_specs=vmem,
        scratch_shapes=[pltpu.VMEM((rows * 4, head_dim), jnp.float32)],
        compiler_params=pltpu.CompilerParams(vmem_limit_bytes=4 * 2**20),
    )(half, own_terms, mine.reshape(-1, head_dim), w_other)
    out_parts = exchange(out_terms.reshape(16, -1, rows), HEADS)
    return jnp.sum(out_parts.astype(jnp.float32), axis=0).astype(jnp.bfloat16).T


def solution(mesh):
    split = Mesh(
        mesh.devices.reshape(8, 4, 2, 2, 2, 2), ("z", "yh", "yl", "core", "xa", "xb")
    )
    placed = (
        P(None, WIDTH + HEADS),
        P(WIDTH, HEADS),
        P(SEQUENCES, None, GROUPS, None),
        P(SEQUENCES, None, GROUPS, None),
        P(SEQUENCES),
        P(HEADS, WIDTH),
    )
    return jax.shard_map(
        shards, mesh=split, in_specs=placed, out_specs=P(None, WIDTH + HEADS), check_vma=False
    )
```
